512 devices in a mesh: vv: 128 (over y, z, core), oo: 4 (over x).
Axes of the slice: x: 4, y: 8, z: 8, core: 2. Of those that a mesh axis runs over, the one named last changes fastest.
Arguments:
- amplitudes: float32 [128, 4, 128, 4096], P(None, 'oo', 'vv'), may hold values from -6 to 6
- tile_len: int32 [16], replicated, may hold values from 40 to 64, as said below
- pair_tiles: int32 [128, 2], P('vv'), may hold values from 0 to 15
- v_blocks: float32 [128, 4, 40, 4096], P('vv'), may hold values from -0.09375 to 0.09375
- block_count: int32 [128], P('vv'), may hold values from 1 to 4, as said below
Outputs:
- ladder: float32 [128, 40, 4, 128], P('vv', None, 'oo')
The draws below stay inside these ranges and needn't reach their ends.
Inputs may be any that keep to these rules, and one draw needn't show every extreme that they name: `tile_len`: some tile is full. `block_count`: some cd tile pair has all 4 slots live.
All inputs are finite; a program needn't handle non-finite values.
Results may differ from the reference program's by a relative error of at most 0.0003.
Values sent between devices are 32-bit elements; how exact they have to be, the bound alone decides.
No kernel may reach another device: no remote copies, remote signals or barrier semaphores. Data moves between devices by JAX's collectives and lax.ppermute only.
A program may use at most 64 MiB of HBM per device.

```python
import jax
import jax.numpy as jnp
from jax import lax

TV = 64
PW = 4096
NTILE = 16
BL = 4
ABW = 40
ROWS_V = 128
ROWS_O = 4
NCD = 128
NAB = 128


def draw_tile_len(key, part):
    key = jax.random.fold_in(key, 11)
    first, second = jax.random.split(key)
    lengths = jax.random.randint(first, (NTILE,), TV - 3 * TV // 8, TV + 1)
    full_tile = jax.random.randint(second, (), 0, NTILE)
    return jnp.where(jnp.arange(NTILE) == full_tile, TV, lengths).astype(jnp.int32)


def draw_block_count(key, part):
    key = jax.random.fold_in(key, 13)
    first, second = jax.random.split(key)
    counts = jax.random.randint(first, (NCD,), 1, BL + 1)
    busiest = jax.random.randint(second, (), 0, NCD)
    return jnp.where(jnp.arange(NCD) == busiest, BL, counts).astype(jnp.int32)


def place_ends(values, key, low, top_value):
    shape = values.shape
    spot = [jax.random.randint(jax.random.fold_in(key, axis), (), 0, shape[axis]) for axis in range(len(shape))]
    values = values.at[tuple(spot)].set(low)
    longest = shape.index(max(shape))
    spot[longest] = (spot[longest] + 1) % shape[longest]
    return values.at[tuple(spot)].set(top_value)


def shard_levels(key, extent, cuts, low, high):
    level = 1.0
    for position, blocks in cuts:
        draws = jax.random.uniform(jax.random.fold_in(jax.random.fold_in(key, 6), position), (blocks,), jnp.float32, low / len(cuts), high / len(cuts))
        level = level * jnp.repeat(jnp.exp(draws), extent[position] // blocks).reshape((-1,) + (1,) * (len(extent) - 1 - position))
    return level


def centred(stream_key, dims, deviation, most, cuts=(), held_as=jnp.bfloat16):
    level = shard_levels(stream_key, dims, cuts, -0.22, 0.18) if cuts else 1.0
    array = jax.random.normal(stream_key, dims, jnp.float32) * deviation * level
    return jnp.minimum(jnp.maximum(array, -most), most).astype(held_as)


def setup_inputs(seed: int = 0) -> dict:
    key_of = jax.random.split(jax.random.key(seed), 6)
    amplitudes = centred(key_of[0], (NCD, ROWS_O, ROWS_V, PW), 1.0, 6.0, ((1, 4), (2, 128)), jnp.float32)
    tile_len = draw_tile_len(jax.random.fold_in(key_of[5], 71), 0)
    pair_tiles = place_ends(jax.random.randint(key_of[2], (NCD, 2), 0, NTILE), jax.random.fold_in(key_of[2], 1), 0, NTILE - 1).astype(jnp.int32)
    v_blocks = centred(key_of[3], (NCD, BL, ABW, PW), PW ** -0.5, 0.09375, ((0, 128),), jnp.float32)
    block_count = draw_block_count(jax.random.fold_in(key_of[5], 71), 0)
    return {"amplitudes": amplitudes, "tile_len": tile_len, "pair_tiles": pair_tiles, "v_blocks": v_blocks, "block_count": block_count}


def reference(amplitudes, tile_len, pair_tiles, v_blocks, block_count):
    highest = lax.Precision.HIGHEST
    pair_index = jnp.arange(TV * TV, dtype=jnp.int32)
    c_index = pair_index // TV
    d_index = pair_index % TV
    ab_tiles = jnp.arange(NAB, dtype=jnp.int32)
    slot_index = jnp.arange(BL, dtype=jnp.int32)
    stride = NAB // BL
    pair_ids = jnp.arange(NCD, dtype=jnp.int32)

    def ladder_step(residual_sum, inputs):
        amp_tile, pair_row, blocks, live_count, pair_id = inputs
        c_length = tile_len[pair_row[0]]
        d_length = tile_len[pair_row[1]]
        cd_mask = ((c_index < c_length) & (d_index < d_length)).astype(jnp.float32)
        amp_rows = (amp_tile * cd_mask).reshape(ROWS_O * ROWS_V, TV * TV)
        products = jnp.einsum("kwe,re->kwr", blocks, amp_rows, precision=highest)
        live_slots = slot_index < live_count
        ab_names = (pair_id + slot_index * stride) % NAB
        one_hot = ((ab_names[:, None] == ab_tiles[None, :]) & live_slots[:, None]).astype(jnp.float32)
        return residual_sum + jnp.einsum("ka,kwr->awr", one_hot, products, precision=highest), None

    start = jnp.zeros((NAB, ABW, ROWS_O * ROWS_V), jnp.float32)
    residual_sum, unused = lax.scan(ladder_step, start, (amplitudes, pair_tiles, v_blocks, block_count, pair_ids))
    return residual_sum.reshape(NAB, ABW, ROWS_O, ROWS_V)
```

```python
import jax
import jax.numpy as jnp
from jax import lax
from jax.experimental import pallas as pl
from jax.experimental.pallas import tpu as pltpu
from jax.sharding import PartitionSpec as P

TV = 64
LANES = 128


def split_blocks(tile_len_ref, pair_ref, count_ref, member_ref, v_ref, out_ref):
    slots, window, width = v_ref.shape
    rows = slots * window
    c_length = tile_len_ref[pair_ref[0, 0]]
    d_length = tile_len_ref[pair_ref[0, 1]]
    count = count_ref[0]
    member = member_ref[0]
    step = 4 * LANES
    for start in range(0, width, step):
        lanes = pl.ds(start, step)
        index = lax.broadcasted_iota(jnp.int32, (window, step), 1) + start
        inside = (index // TV < c_length) & (index % TV < d_length)
        blocks = []
        for target in range(slots):
            slot = lax.rem(target - member + slots, slots)
            live = jnp.where(slot < count, 1, 0)
            blocks.append(jnp.where(inside & (live > 0), v_ref[slot, :, lanes], 0.0))
        block = jnp.concatenate(blocks, axis=0)
        head = block.astype(jnp.bfloat16)
        out_ref[0:rows, lanes] = head
        out_ref[rows : 2 * rows, lanes] = (block - head.astype(jnp.float32)).astype(jnp.bfloat16)


def contract(v_ref, amp_ref, out_ref, split_ref):
    rows = out_ref.shape[1]
    depth = amp_ref.shape[0] // rows
    for j in range(depth):
        part = amp_ref[pl.ds(j, rows, stride=depth), :]
        head = part.astype(jnp.bfloat16)
        tail = (part - head.astype(jnp.float32)).astype(jnp.bfloat16)
        lanes = pl.ds(j * LANES, LANES)
        split_ref[0:rows, lanes] = head
        split_ref[rows : 2 * rows, lanes] = tail
    both = lax.dot_general(
        v_ref[...], split_ref[...], (((1,), (1,)), ((), ())), preferred_element_type=jnp.float32
    )
    half = out_ref.shape[0]
    out_ref[...] = (both[half:, rows:] + both[half:, :rows] + both[:half, rows:]) + both[:half, :rows]


def shards(amplitudes, tile_len, pair_tiles, v_blocks, block_count):
    owners = lax.axis_size("vv")
    slots, window, width = v_blocks.shape[1:]
    stride = owners // slots
    depth = width // LANES
    rows = amplitudes.shape[0]
    arrived = lax.all_to_all(
        amplitudes.reshape(rows, depth, LANES), "vv", split_axis=0, concat_axis=0, tiled=True
    )

    member = lax.axis_index("vv") // stride
    v_split = pl.pallas_call(
        split_blocks,
        out_shape=jax.ShapeDtypeStruct((2 * slots * window, width), jnp.bfloat16),
        in_specs=[pl.BlockSpec(memory_space=pltpu.SMEM)] * 4 + [pl.BlockSpec(memory_space=pltpu.VMEM)],
        out_specs=pl.BlockSpec(memory_space=pltpu.VMEM),
        compiler_params=pltpu.CompilerParams(vmem_limit_bytes=24 * 1024 * 1024),
        cost_estimate=pl.CostEstimate(
            flops=8 * slots * window * width, bytes_accessed=8 * slots * window * width, transcendentals=0
        ),
        name="split_blocks",
    )(tile_len, pair_tiles, block_count, member.astype(jnp.int32)[None], v_blocks[0])

    terms = pl.pallas_call(
        contract,
        out_shape=jax.ShapeDtypeStruct((slots * window, rows), jnp.float32),
        in_specs=[pl.BlockSpec(memory_space=pltpu.VMEM)] * 2,
        out_specs=pl.BlockSpec(memory_space=pltpu.VMEM),
        scratch_shapes=[pltpu.VMEM((2 * rows, width), jnp.bfloat16)],
        compiler_params=pltpu.CompilerParams(vmem_limit_bytes=32 * 1024 * 1024),
        cost_estimate=pl.CostEstimate(
            flops=8 * slots * window * rows * width, bytes_accessed=6 * rows * width, transcendentals=0
        ),
        name="contract",
    )(v_split, arrived.reshape(rows * depth, LANES))

    groups = [[i + stride * k for k in range(slots)] for i in range(stride)]
    moved = lax.all_to_all(
        terms.reshape(slots, window, rows), "vv", split_axis=0, concat_axis=0, axis_index_groups=groups, tiled=True
    )
    total = (moved[0] + moved[1]) + (moved[2] + moved[3])
    return total.reshape(1, window, 1, rows)


def solution(mesh):
    return jax.shard_map(
        shards,
        mesh=mesh,
        in_specs=(
            P(None, "oo", "vv", None),
            P(),
            P("vv", None),
            P("vv", None, None, None),
            P("vv"),
        ),
        out_specs=P("vv", None, "oo", None),
        check_vma=False,
    )
```

```python
import jax
import jax.numpy as jnp
from jax import lax
from jax.experimental import pallas as pl
from jax.experimental.pallas import tpu as pltpu
from jax.sharding import PartitionSpec as P

TV = 64
LANES = 128


def split_blocks(tile_len_ref, pair_ref, count_ref, member_ref, v_ref, head_ref, tail_ref):
    slots, window, width = v_ref.shape
    c_length = tile_len_ref[pair_ref[0, 0]]
    d_length = tile_len_ref[pair_ref[0, 1]]
    count = count_ref[0]
    member = member_ref[0]
    step = 4 * LANES
    for start in range(0, width, step):
        lanes = pl.ds(start, step)
        index = lax.broadcasted_iota(jnp.int32, (window, step), 1) + start
        inside = (index // TV < c_length) & (index % TV < d_length)
        blocks = []
        for target in range(slots):
            slot = lax.rem(target - member + slots, slots)
            live = jnp.where(slot < count, 1, 0)
            blocks.append(jnp.where(inside & (live > 0), v_ref[slot, :, lanes], 0.0))
        block = jnp.concatenate(blocks, axis=0)
        head = block.astype(jnp.bfloat16)
        head_ref[:, lanes] = head
        tail_ref[:, lanes] = (block - head.astype(jnp.float32)).astype(jnp.bfloat16)


def times_transposed(a, b):
    return lax.dot_general(a, b, (((1,), (1,)), ((), ())), preferred_element_type=jnp.float32)


def contract(head_ref, tail_hbm, amp_ref, out_ref, tail_ref, split_ref, sem):
    copy = pltpu.make_async_copy(tail_hbm, tail_ref, sem)
    copy.start()
    rows = out_ref.shape[1]
    depth = amp_ref.shape[0] // rows
    for j in range(depth):
        part = amp_ref[pl.ds(j, rows, stride=depth), :]
        head = part.astype(jnp.bfloat16)
        tail = (part - head.astype(jnp.float32)).astype(jnp.bfloat16)
        lanes = pl.ds(j * LANES, LANES)
        split_ref[0:rows, lanes] = head
        split_ref[rows : 2 * rows, lanes] = tail
    upper = times_transposed(head_ref[...], split_ref[...])
    copy.wait()
    lower = times_transposed(tail_ref[...], split_ref[...])
    out_ref[...] = (lower[:, rows:] + lower[:, :rows] + upper[:, rows:]) + upper[:, :rows]


def shards(amplitudes, tile_len, pair_tiles, v_blocks, block_count):
    owners = lax.axis_size("vv")
    slots, window, width = v_blocks.shape[1:]
    stride = owners // slots
    depth = width // LANES
    rows = amplitudes.shape[0]
    arrived = lax.all_to_all(
        amplitudes.reshape(rows, depth, LANES), "vv", split_axis=0, concat_axis=0, tiled=True
    )

    member = lax.axis_index("vv") // stride
    heads, tails = pl.pallas_call(
        split_blocks,
        out_shape=[
            jax.ShapeDtypeStruct((slots * window, width), jnp.bfloat16),
            pltpu.HBM((slots * window, width), jnp.bfloat16),
        ],
        in_specs=[pl.BlockSpec(memory_space=pltpu.SMEM)] * 4 + [pl.BlockSpec(memory_space=pltpu.VMEM)],
        out_specs=[pl.BlockSpec(memory_space=pltpu.VMEM)] * 2,
        compiler_params=pltpu.CompilerParams(vmem_limit_bytes=16 * 1024 * 1024),
        cost_estimate=pl.CostEstimate(
            flops=8 * slots * window * width, bytes_accessed=8 * slots * window * width, transcendentals=0
        ),
        name="split_blocks",
    )(tile_len, pair_tiles, block_count, member.astype(jnp.int32)[None], v_blocks[0])

    terms = pl.pallas_call(
        contract,
        out_shape=jax.ShapeDtypeStruct((slots * window, rows), jnp.float32),
        in_specs=[
            pl.BlockSpec(memory_space=pltpu.VMEM),
            pl.BlockSpec(memory_space=pl.ANY),
            pl.BlockSpec(memory_space=pltpu.VMEM),
        ],
        out_specs=pl.BlockSpec(memory_space=pltpu.VMEM),
        scratch_shapes=[
            pltpu.VMEM((slots * window, width), jnp.bfloat16),
            pltpu.VMEM((2 * rows, width), jnp.bfloat16),
            pltpu.SemaphoreType.DMA,
        ],
        compiler_params=pltpu.CompilerParams(vmem_limit_bytes=16 * 1024 * 1024),
        cost_estimate=pl.CostEstimate(
            flops=8 * slots * window * rows * width, bytes_accessed=6 * rows * width, transcendentals=0
        ),
        name="contract",
    )(heads, pltpu.with_memory_space_constraint(tails, pltpu.HBM), arrived.reshape(rows * depth, LANES))

    groups = [[i + stride * k for k in range(slots)] for i in range(stride)]
    moved = lax.all_to_all(
        terms.reshape(slots, window, rows), "vv", split_axis=0, concat_axis=0, axis_index_groups=groups, tiled=True
    )
    total = (moved[0] + moved[1]) + (moved[2] + moved[3])
    return total.reshape(1, window, 1, rows)


def solution(mesh):
    return jax.shard_map(
        shards,
        mesh=mesh,
        in_specs=(
            P(None, "oo", "vv", None),
            P(),
            P("vv", None),
            P("vv", None, None, None),
            P("vv"),
        ),
        out_specs=P("vv", None, "oo", None),
        check_vma=False,
    )
```

```python
import jax
import jax.numpy as jnp
from jax import lax
from jax.experimental import pallas as pl
from jax.experimental.pallas import tpu as pltpu
from jax.sharding import PartitionSpec as P

TV = 64
LANES = 128
CHUNKS = 2


def split_blocks(tile_len_ref, pair_ref, count_ref, member_ref, v_ref, head_ref, tail_ref):
    slots, window, width = v_ref.shape
    c_length = tile_len_ref[pair_ref[0, 0]]
    d_length = tile_len_ref[pair_ref[0, 1]]
    count = count_ref[0]
    member = member_ref[0]
    step = 4 * LANES
    for start in range(0, width, step):
        lanes = pl.ds(start, step)
        index = lax.broadcasted_iota(jnp.int32, (window, step), 1) + start
        inside = (index // TV < c_length) & (index % TV < d_length)
        blocks = []
        for target in range(slots):
            slot = lax.rem(target - member + slots, slots)
            live = jnp.where(slot < count, 1, 0)
            blocks.append(jnp.where(inside & (live > 0), v_ref[slot, :, lanes], 0.0))
        block = jnp.concatenate(blocks, axis=0)
        head = block.astype(jnp.bfloat16)
        head_ref[:, lanes] = head
        tail_ref[:, lanes] = (block - head.astype(jnp.float32)).astype(jnp.bfloat16)


def times_transposed(a, b):
    return lax.dot_general(a, b, (((1,), (1,)), ((), ())), preferred_element_type=jnp.float32)


def contract(head_ref, tail_hbm, amp_ref, out_ref, tail_ref, sem):
    copy = pltpu.make_async_copy(tail_hbm, tail_ref, sem)
    copy.start()
    half, rows = out_ref.shape
    depth = amp_ref.shape[0] // rows
    chunk = depth // CHUNKS
    both = None
    for start in range(0, depth, chunk):
        heads, tails = [], []
        for j in range(start, start + chunk):
            part = amp_ref[pl.ds(j, rows, stride=depth), :]
            heads.append(part.astype(jnp.bfloat16))
            tails.append((part - heads[-1].astype(jnp.float32)).astype(jnp.bfloat16))
        amp = jnp.concatenate([jnp.concatenate(heads, axis=1), jnp.concatenate(tails, axis=1)], axis=0)
        if start == 0:
            copy.wait()
        lanes = pl.ds(start * LANES, chunk * LANES)
        blocks = jnp.concatenate([head_ref[:, lanes], tail_ref[:, lanes]], axis=0)
        product = times_transposed(blocks, amp)
        both = product if both is None else both + product
    out_ref[...] = (both[half:, rows:] + both[half:, :rows] + both[:half, rows:]) + both[:half, :rows]


def shards(amplitudes, tile_len, pair_tiles, v_blocks, block_count):
    owners = lax.axis_size("vv")
    slots, window, width = v_blocks.shape[1:]
    stride = owners // slots
    depth = width // LANES
    rows = amplitudes.shape[0]
    arrived = lax.all_to_all(
        amplitudes.reshape(rows, depth, LANES), "vv", split_axis=0, concat_axis=0, tiled=True
    )

    member = lax.axis_index("vv") // stride
    heads, tails = pl.pallas_call(
        split_blocks,
        out_shape=[
            jax.ShapeDtypeStruct((slots * window, width), jnp.bfloat16),
            pltpu.HBM((slots * window, width), jnp.bfloat16),
        ],
        in_specs=[pl.BlockSpec(memory_space=pltpu.SMEM)] * 4 + [pl.BlockSpec(memory_space=pltpu.VMEM)],
        out_specs=[pl.BlockSpec(memory_space=pltpu.VMEM)] * 2,
        compiler_params=pltpu.CompilerParams(vmem_limit_bytes=16 * 1024 * 1024),
        cost_estimate=pl.CostEstimate(
            flops=8 * slots * window * width, bytes_accessed=8 * slots * window * width, transcendentals=0
        ),
        name="split_blocks",
    )(tile_len, pair_tiles, block_count, member.astype(jnp.int32)[None], v_blocks[0])

    terms = pl.pallas_call(
        contract,
        out_shape=jax.ShapeDtypeStruct((slots * window, rows), jnp.float32),
        in_specs=[
            pl.BlockSpec(memory_space=pltpu.VMEM),
            pl.BlockSpec(memory_space=pl.ANY),
            pl.BlockSpec(memory_space=pltpu.VMEM),
        ],
        out_specs=pl.BlockSpec(memory_space=pltpu.VMEM),
        scratch_shapes=[
            pltpu.VMEM((slots * window, width), jnp.bfloat16),
            pltpu.SemaphoreType.DMA,
        ],
        compiler_params=pltpu.CompilerParams(vmem_limit_bytes=16 * 1024 * 1024),
        cost_estimate=pl.CostEstimate(
            flops=8 * slots * window * rows * width, bytes_accessed=6 * rows * width, transcendentals=0
        ),
        name="contract",
    )(heads, pltpu.with_memory_space_constraint(tails, pltpu.HBM), arrived.reshape(rows * depth, LANES))

    groups = [[i + stride * k for k in range(slots)] for i in range(stride)]
    moved = lax.all_to_all(
        terms.reshape(slots, window, rows), "vv", split_axis=0, concat_axis=0, axis_index_groups=groups, tiled=True
    )
    total = (moved[0] + moved[1]) + (moved[2] + moved[3])
    return total.reshape(1, window, 1, rows)


def solution(mesh):
    return jax.shard_map(
        shards,
        mesh=mesh,
        in_specs=(
            P(None, "oo", "vv", None),
            P(),
            P("vv", None),
            P("vv", None, None, None),
            P("vv"),
        ),
        out_specs=P("vv", None, "oo", None),
        check_vma=False,
    )
```

```python
import jax
import jax.numpy as jnp
from jax import lax
from jax.experimental import pallas as pl
from jax.experimental.pallas import tpu as pltpu
from jax.sharding import PartitionSpec as P

TV = 64
LANES = 128
CHUNKS = 2


def split_blocks(tile_len_ref, pair_ref, count_ref, v_ref, head_ref, tail_ref):
    slots, window, width = v_ref.shape
    c_length = tile_len_ref[pair_ref[0, 0]]
    d_length = tile_len_ref[pair_ref[0, 1]]
    count = count_ref[0]
    step = 4 * LANES
    for start in range(0, width, step):
        lanes = pl.ds(start, step)
        index = lax.broadcasted_iota(jnp.int32, (window, step), 1) + start
        inside = (index // TV < c_length) & (index % TV < d_length)
        blocks = []
        for slot in range(slots):
            live = jnp.where(slot < count, 1, 0)
            blocks.append(jnp.where(inside & (live > 0), v_ref[slot, :, lanes], 0.0))
        block = jnp.concatenate(blocks, axis=0)
        head = block.astype(jnp.bfloat16)
        head_ref[:, lanes] = head
        tail_ref[:, lanes] = (block - head.astype(jnp.float32)).astype(jnp.bfloat16)


def times_transposed(a, b):
    return lax.dot_general(a, b, (((1,), (1,)), ((), ())), preferred_element_type=jnp.float32)


def contract(head_ref, tail_hbm, amp_ref, *refs):
    *out_refs, tail_ref, sem = refs
    copy = pltpu.make_async_copy(tail_hbm, tail_ref, sem)
    copy.start()
    window, rows = out_refs[0].shape
    half = window * len(out_refs)
    depth = amp_ref.shape[0] // rows
    chunk = depth // CHUNKS
    both = None
    for start in range(0, depth, chunk):
        heads, tails = [], []
        for j in range(start, start + chunk):
            part = amp_ref[pl.ds(j, rows, stride=depth), :]
            heads.append(part.astype(jnp.bfloat16))
            tails.append((part - heads[-1].astype(jnp.float32)).astype(jnp.bfloat16))
        amp = jnp.concatenate([jnp.concatenate(heads, axis=1), jnp.concatenate(tails, axis=1)], axis=0)
        if start == 0:
            copy.wait()
        lanes = pl.ds(start * LANES, chunk * LANES)
        blocks = jnp.concatenate([head_ref[:, lanes], tail_ref[:, lanes]], axis=0)
        product = times_transposed(blocks, amp)
        both = product if both is None else both + product
    total = (both[half:, rows:] + both[half:, :rows] + both[:half, rows:]) + both[:half, :rows]
    for slot, out_ref in enumerate(out_refs):
        out_ref[...] = total[slot * window : (slot + 1) * window]


def shards(amplitudes, tile_len, pair_tiles, v_blocks, block_count):
    owners = lax.axis_size("vv")
    slots, window, width = v_blocks.shape[1:]
    stride = owners // slots
    depth = width // LANES
    rows = amplitudes.shape[0]
    arrived = lax.all_to_all(
        amplitudes.reshape(rows, depth, LANES), "vv", split_axis=0, concat_axis=0, tiled=True
    )

    heads, tails = pl.pallas_call(
        split_blocks,
        out_shape=[
            jax.ShapeDtypeStruct((slots * window, width), jnp.bfloat16),
            pltpu.HBM((slots * window, width), jnp.bfloat16),
        ],
        in_specs=[pl.BlockSpec(memory_space=pltpu.SMEM)] * 3 + [pl.BlockSpec(memory_space=pltpu.VMEM)],
        out_specs=[pl.BlockSpec(memory_space=pltpu.VMEM)] * 2,
        compiler_params=pltpu.CompilerParams(vmem_limit_bytes=16 * 1024 * 1024),
        cost_estimate=pl.CostEstimate(
            flops=8 * slots * window * width, bytes_accessed=8 * slots * window * width, transcendentals=0
        ),
        name="split_blocks",
    )(tile_len, pair_tiles, block_count, v_blocks[0])

    terms = pl.pallas_call(
        contract,
        out_shape=[jax.ShapeDtypeStruct((window, rows), jnp.float32)] * slots,
        in_specs=[
            pl.BlockSpec(memory_space=pltpu.VMEM),
            pl.BlockSpec(memory_space=pl.ANY),
            pl.BlockSpec(memory_space=pltpu.VMEM),
        ],
        out_specs=[pl.BlockSpec(memory_space=pltpu.VMEM)] * slots,
        scratch_shapes=[
            pltpu.VMEM((slots * window, width), jnp.bfloat16),
            pltpu.SemaphoreType.DMA,
        ],
        compiler_params=pltpu.CompilerParams(vmem_limit_bytes=16 * 1024 * 1024),
        cost_estimate=pl.CostEstimate(
            flops=8 * slots * window * rows * width, bytes_accessed=6 * rows * width, transcendentals=0
        ),
        name="contract",
    )(heads, pltpu.with_memory_space_constraint(tails, pltpu.HBM), arrived.reshape(rows * depth, LANES))

    moved = {}
    for slot in sorted(range(1, slots), key=lambda k: abs(k - slots // 2)):
        route = [(i, (i + slot * stride) % owners) for i in range(owners)]
        moved[slot] = lax.ppermute(terms[slot], "vv", route)
    total = terms[0]
    for slot in range(1, slots):
        total = total + moved[slot]
    return total.reshape(1, window, 1, rows)


def solution(mesh):
    return jax.shard_map(
        shards,
        mesh=mesh,
        in_specs=(
            P(None, "oo", "vv", None),
            P(),
            P("vv", None),
            P("vv", None, None, None),
            P("vv"),
        ),
        out_specs=P("vv", None, "oo", None),
        check_vma=False,
    )
```

```python
import jax
import jax.numpy as jnp
from jax import lax
from jax.experimental import pallas as pl
from jax.experimental.pallas import tpu as pltpu
from jax.sharding import PartitionSpec as P

TV = 64
LANES = 128
CHUNKS = 2


def split_blocks(tile_len_ref, pair_ref, count_ref, member_ref, v_ref, head_ref, tail_ref, own_ref):
    slots, window, width = v_ref.shape
    c_length = tile_len_ref[pair_ref[0, 0]]
    d_length = tile_len_ref[pair_ref[0, 1]]
    count = count_ref[0]
    member = member_ref[0]
    step = 4 * LANES
    for start in range(0, width, step):
        lanes = pl.ds(start, step)
        index = lax.broadcasted_iota(jnp.int32, (window, step), 1) + start
        inside = (index // TV < c_length) & (index % TV < d_length)
        blocks = []
        for target in range(slots):
            slot = lax.rem(target - member + slots, slots)
            live = jnp.where((slot < count) & (slot > 0), 1, 0)
            blocks.append(jnp.where(inside & (live > 0), v_ref[slot, :, lanes], 0.0))
        block = jnp.concatenate(blocks, axis=0)
        head = block.astype(jnp.bfloat16)
        head_ref[:, lanes] = head
        tail_ref[:, lanes] = (block - head.astype(jnp.float32)).astype(jnp.bfloat16)
        own = jnp.where(inside & (count > 0), v_ref[0, :, lanes], 0.0)
        above = own.astype(jnp.bfloat16).astype(jnp.float32)
        own_ref[:, lanes] = jnp.concatenate([above, own - above], axis=0).astype(jnp.bfloat16)


def times_transposed(a, b):
    return lax.dot_general(a, b, (((1,), (1,)), ((), ())), preferred_element_type=jnp.float32)


def contract(head_ref, tail_hbm, amp_ref, out_ref, tail_ref, sem):
    copy = pltpu.make_async_copy(tail_hbm, tail_ref, sem)
    copy.start()
    half, rows = out_ref.shape
    depth = amp_ref.shape[0] // rows
    chunk = depth // CHUNKS
    both = None
    for start in range(0, depth, chunk):
        heads, tails = [], []
        for j in range(start, start + chunk):
            part = amp_ref[pl.ds(j, rows, stride=depth), :]
            heads.append(part.astype(jnp.bfloat16))
            tails.append((part - heads[-1].astype(jnp.float32)).astype(jnp.bfloat16))
        amp = jnp.concatenate([jnp.concatenate(heads, axis=1), jnp.concatenate(tails, axis=1)], axis=0)
        if start == 0:
            copy.wait()
        lanes = pl.ds(start * LANES, chunk * LANES)
        blocks = jnp.concatenate([head_ref[:, lanes], tail_ref[:, lanes]], axis=0)
        product = times_transposed(blocks, amp)
        both = product if both is None else both + product
    out_ref[...] = (both[half:, rows:] + both[half:, :rows] + both[:half, rows:]) + both[:half, :rows]


def contract_own(own_ref, amp_ref, out_ref):
    window, rows = out_ref.shape
    depth = amp_ref.shape[0] // rows
    chunk = depth // CHUNKS
    both = None
    for start in range(0, depth, chunk):
        heads, tails = [], []
        for j in range(start, start + chunk):
            part = amp_ref[pl.ds(j, rows, stride=depth), :]
            heads.append(part.astype(jnp.bfloat16))
            tails.append((part - heads[-1].astype(jnp.float32)).astype(jnp.bfloat16))
        amp = jnp.concatenate([jnp.concatenate(heads, axis=1), jnp.concatenate(tails, axis=1)], axis=0)
        product = times_transposed(own_ref[:, pl.ds(start * LANES, chunk * LANES)], amp)
        both = product if both is None else both + product
    out_ref[...] = (both[window:, rows:] + both[window:, :rows] + both[:window, rows:]) + both[:window, :rows]


def shards(amplitudes, tile_len, pair_tiles, v_blocks, block_count):
    owners = lax.axis_size("vv")
    slots, window, width = v_blocks.shape[1:]
    stride = owners // slots
    depth = width // LANES
    rows = amplitudes.shape[0]
    arrived = lax.all_to_all(
        amplitudes.reshape(rows, depth, LANES), "vv", split_axis=0, concat_axis=0, tiled=True
    )

    member = lax.axis_index("vv") // stride
    heads, tails, own = pl.pallas_call(
        split_blocks,
        out_shape=[
            jax.ShapeDtypeStruct((slots * window, width), jnp.bfloat16),
            pltpu.HBM((slots * window, width), jnp.bfloat16),
            pltpu.HBM((2 * window, width), jnp.bfloat16),
        ],
        in_specs=[pl.BlockSpec(memory_space=pltpu.SMEM)] * 4 + [pl.BlockSpec(memory_space=pltpu.VMEM)],
        out_specs=[pl.BlockSpec(memory_space=pltpu.VMEM)] * 3,
        compiler_params=pltpu.CompilerParams(vmem_limit_bytes=16 * 1024 * 1024),
        cost_estimate=pl.CostEstimate(
            flops=8 * slots * window * width, bytes_accessed=8 * slots * window * width, transcendentals=0
        ),
        name="split_blocks",
    )(tile_len, pair_tiles, block_count, member.astype(jnp.int32)[None], v_blocks[0])

    terms = pl.pallas_call(
        contract,
        out_shape=jax.ShapeDtypeStruct((slots * window, rows), jnp.float32),
        in_specs=[
            pl.BlockSpec(memory_space=pltpu.VMEM),
            pl.BlockSpec(memory_space=pl.ANY),
            pl.BlockSpec(memory_space=pltpu.VMEM),
        ],
        out_specs=pl.BlockSpec(memory_space=pltpu.VMEM),
        scratch_shapes=[
            pltpu.VMEM((slots * window, width), jnp.bfloat16),
            pltpu.SemaphoreType.DMA,
        ],
        compiler_params=pltpu.CompilerParams(vmem_limit_bytes=16 * 1024 * 1024),
        cost_estimate=pl.CostEstimate(
            flops=8 * slots * window * rows * width, bytes_accessed=6 * rows * width, transcendentals=0
        ),
        name="contract",
    )(heads, pltpu.with_memory_space_constraint(tails, pltpu.HBM), arrived.reshape(rows * depth, LANES))

    mine = pl.pallas_call(
        contract_own,
        out_shape=jax.ShapeDtypeStruct((window, rows), jnp.float32),
        in_specs=[pl.BlockSpec(memory_space=pltpu.VMEM)] * 2,
        out_specs=pl.BlockSpec(memory_space=pltpu.VMEM),
        compiler_params=pltpu.CompilerParams(vmem_limit_bytes=16 * 1024 * 1024),
        cost_estimate=pl.CostEstimate(
            flops=8 * slots * window * rows * width, bytes_accessed=6 * rows * width, transcendentals=0
        ),
        name="contract_own",
    )(own, arrived.reshape(rows * depth, LANES))

    groups = [[i + stride * k for k in range(slots)] for i in range(stride)]
    moved = lax.all_to_all(
        terms.reshape(slots, window, rows), "vv", split_axis=0, concat_axis=0, axis_index_groups=groups, tiled=True
    )
    total = ((moved[0] + moved[1]) + (moved[2] + moved[3])) + mine
    return total.reshape(1, window, 1, rows)


def solution(mesh):
    return jax.shard_map(
        shards,
        mesh=mesh,
        in_specs=(
            P(None, "oo", "vv", None),
            P(),
            P("vv", None),
            P("vv", None, None, None),
            P("vv"),
        ),
        out_specs=P("vv", None, "oo", None),
        check_vma=False,
    )
```

```python
import jax
import jax.numpy as jnp
from jax import lax
from jax.experimental import pallas as pl
from jax.experimental.pallas import tpu as pltpu
from jax.sharding import PartitionSpec as P

TV = 64
LANES = 128
CHUNKS = 2


def split_blocks(tile_len_ref, pair_ref, count_ref, v_ref, head_ref, tail_ref, own_ref):
    slots, window, width = v_ref.shape
    c_length = tile_len_ref[pair_ref[0, 0]]
    d_length = tile_len_ref[pair_ref[0, 1]]
    count = count_ref[0]
    step = 4 * LANES
    spare = head_ref.shape[0] - (slots - 1) * window
    for start in range(0, width, step):
        lanes = pl.ds(start, step)
        index = lax.broadcasted_iota(jnp.int32, (window, step), 1) + start
        inside = (index // TV < c_length) & (index % TV < d_length)
        kept = []
        for slot in range(slots):
            live = jnp.where(slot < count, 1, 0)
            kept.append(jnp.where(inside & (live > 0), v_ref[slot, :, lanes], 0.0))
        padding = [jnp.zeros((spare, step), jnp.float32)] if spare else []
        block = jnp.concatenate(kept[1:] + padding, axis=0)
        head = block.astype(jnp.bfloat16)
        head_ref[:, lanes] = head
        tail_ref[:, lanes] = (block - head.astype(jnp.float32)).astype(jnp.bfloat16)
        above = kept[0].astype(jnp.bfloat16).astype(jnp.float32)
        own_ref[:, lanes] = jnp.concatenate([above, kept[0] - above], axis=0).astype(jnp.bfloat16)


def times_transposed(a, b):
    return lax.dot_general(a, b, (((1,), (1,)), ((), ())), preferred_element_type=jnp.float32)


def contract(member_ref, head_ref, tail_hbm, amp_ref, out_ref, tail_ref, sem):
    copy = pltpu.make_async_copy(tail_hbm, tail_ref, sem)
    copy.start()
    slots, window, rows = out_ref.shape
    half = head_ref.shape[0]
    depth = amp_ref.shape[0] // rows
    chunk = depth // CHUNKS
    both = None
    for start in range(0, depth, chunk):
        heads, tails = [], []
        for j in range(start, start + chunk):
            part = amp_ref[pl.ds(j, rows, stride=depth), :]
            heads.append(part.astype(jnp.bfloat16))
            tails.append((part - heads[-1].astype(jnp.float32)).astype(jnp.bfloat16))
        amp = jnp.concatenate([jnp.concatenate(heads, axis=1), jnp.concatenate(tails, axis=1)], axis=0)
        if start == 0:
            copy.wait()
        lanes = pl.ds(start * LANES, chunk * LANES)
        blocks = jnp.concatenate([head_ref[:, lanes], tail_ref[:, lanes]], axis=0)
        product = times_transposed(blocks, amp)
        both = product if both is None else both + product
    total = (both[half:, rows:] + both[half:, :rows] + both[:half, rows:]) + both[:half, :rows]
    member = member_ref[0]
    out_ref[member] = jnp.zeros((window, rows), jnp.float32)
    for slot in range(1, slots):
        out_ref[lax.rem(member + slot, slots)] = total[(slot - 1) * window : slot * window]


def contract_own(own_ref, amp_ref, out_ref):
    window, rows = out_ref.shape
    depth = amp_ref.shape[0] // rows
    chunk = depth // CHUNKS
    both = None
    for start in range(0, depth, chunk):
        heads, tails = [], []
        for j in range(start, start + chunk):
            part = amp_ref[pl.ds(j, rows, stride=depth), :]
            heads.append(part.astype(jnp.bfloat16))
            tails.append((part - heads[-1].astype(jnp.float32)).astype(jnp.bfloat16))
        amp = jnp.concatenate([jnp.concatenate(heads, axis=1), jnp.concatenate(tails, axis=1)], axis=0)
        product = times_transposed(own_ref[:, pl.ds(start * LANES, chunk * LANES)], amp)
        both = product if both is None else both + product
    out_ref[...] = (both[window:, rows:] + both[window:, :rows] + both[:window, rows:]) + both[:window, :rows]


def shards(amplitudes, tile_len, pair_tiles, v_blocks, block_count):
    owners = lax.axis_size("vv")
    slots, window, width = v_blocks.shape[1:]
    stride = owners // slots
    depth = width // LANES
    rows = amplitudes.shape[0]
    arrived = lax.all_to_all(
        amplitudes.reshape(rows, depth, LANES), "vv", split_axis=0, concat_axis=0, tiled=True
    )

    member = lax.axis_index("vv") // stride
    remote = -(-(slots - 1) * window // 16) * 16
    heads, tails, own = pl.pallas_call(
        split_blocks,
        out_shape=[
            jax.ShapeDtypeStruct((remote, width), jnp.bfloat16),
            pltpu.HBM((remote, width), jnp.bfloat16),
            pltpu.HBM((2 * window, width), jnp.bfloat16),
        ],
        in_specs=[pl.BlockSpec(memory_space=pltpu.SMEM)] * 3 + [pl.BlockSpec(memory_space=pltpu.VMEM)],
        out_specs=[pl.BlockSpec(memory_space=pltpu.VMEM)] * 3,
        compiler_params=pltpu.CompilerParams(vmem_limit_bytes=16 * 1024 * 1024),
        cost_estimate=pl.CostEstimate(
            flops=8 * slots * window * width, bytes_accessed=8 * slots * window * width, transcendentals=0
        ),
        name="split_blocks",
    )(tile_len, pair_tiles, block_count, v_blocks[0])

    terms = pl.pallas_call(
        contract,
        out_shape=pltpu.VMEM((slots, window, rows), jnp.float32),
        in_specs=[
            pl.BlockSpec(memory_space=pltpu.SMEM),
            pl.BlockSpec(memory_space=pltpu.VMEM),
            pl.BlockSpec(memory_space=pl.ANY),
            pl.BlockSpec(memory_space=pltpu.VMEM),
        ],
        out_specs=pl.BlockSpec(memory_space=pltpu.VMEM),
        scratch_shapes=[pltpu.VMEM((remote, width), jnp.bfloat16), pltpu.SemaphoreType.DMA],
        compiler_params=pltpu.CompilerParams(vmem_limit_bytes=16 * 1024 * 1024),
        cost_estimate=pl.CostEstimate(
            flops=8 * slots * window * rows * width, bytes_accessed=6 * rows * width, transcendentals=0
        ),
        name="contract",
    )(
        member.astype(jnp.int32)[None],
        heads,
        pltpu.with_memory_space_constraint(tails, pltpu.HBM),
        arrived.reshape(rows * depth, LANES),
    )

    mine = pl.pallas_call(
        contract_own,
        out_shape=jax.ShapeDtypeStruct((window, rows), jnp.float32),
        in_specs=[pl.BlockSpec(memory_space=pltpu.VMEM)] * 2,
        out_specs=pl.BlockSpec(memory_space=pltpu.VMEM),
        compiler_params=pltpu.CompilerParams(vmem_limit_bytes=16 * 1024 * 1024),
        cost_estimate=pl.CostEstimate(
            flops=8 * slots * window * rows * width, bytes_accessed=6 * rows * width, transcendentals=0
        ),
        name="contract_own",
    )(own, arrived.reshape(rows * depth, LANES))

    groups = [[i + stride * k for k in range(slots)] for i in range(stride)]
    moved = lax.all_to_all(
        terms, "vv", split_axis=0, concat_axis=0, axis_index_groups=groups, tiled=True
    )
    total = ((moved[0] + moved[1]) + (moved[2] + moved[3])) + mine
    return total.reshape(1, window, 1, rows)


def solution(mesh):
    return jax.shard_map(
        shards,
        mesh=mesh,
        in_specs=(
            P(None, "oo", "vv", None),
            P(),
            P("vv", None),
            P("vv", None, None, None),
            P("vv"),
        ),
        out_specs=P("vv", None, "oo", None),
        check_vma=False,
    )
```

```python
import jax
import jax.numpy as jnp
from jax import lax
from jax.experimental import pallas as pl
from jax.experimental.pallas import tpu as pltpu
from jax.sharding import PartitionSpec as P

TV = 64
LANES = 128
FIRST = 11 / 16


def split_blocks(tile_len_ref, pair_ref, count_ref, member_ref, v_ref, head_ref, tail_ref):
    slots, window, width = v_ref.shape
    c_length = tile_len_ref[pair_ref[0, 0]]
    d_length = tile_len_ref[pair_ref[0, 1]]
    count = count_ref[0]
    member = member_ref[0]
    step = 4 * LANES
    for start in range(0, width, step):
        lanes = pl.ds(start, step)
        index = lax.broadcasted_iota(jnp.int32, (window, step), 1) + start
        inside = (index // TV < c_length) & (index % TV < d_length)
        blocks = []
        for target in range(slots):
            slot = lax.rem(target - member + slots, slots)
            live = jnp.where(slot < count, 1, 0)
            blocks.append(jnp.where(inside & (live > 0), v_ref[slot, :, lanes], 0.0))
        block = jnp.concatenate(blocks, axis=0)
        head = block.astype(jnp.bfloat16)
        head_ref[:, lanes] = head
        tail_ref[:, lanes] = (block - head.astype(jnp.float32)).astype(jnp.bfloat16)


def times_transposed(a, b):
    return lax.dot_general(a, b, (((1,), (1,)), ((), ())), preferred_element_type=jnp.float32)


def contract(head_ref, tail_hbm, amp_ref, out_ref, tail_ref, sem):
    copy = pltpu.make_async_copy(tail_hbm, tail_ref, sem)
    copy.start()
    half, rows = out_ref.shape
    depth = amp_ref.shape[0] // rows
    cut = int(depth * FIRST)
    both = None
    for start, end in ((0, cut), (cut, depth)):
        heads, tails = [], []
        for j in range(start, end):
            part = amp_ref[pl.ds(j, rows, stride=depth), :]
            heads.append(part.astype(jnp.bfloat16))
            tails.append((part - heads[-1].astype(jnp.float32)).astype(jnp.bfloat16))
        amp = jnp.concatenate([jnp.concatenate(heads, axis=1), jnp.concatenate(tails, axis=1)], axis=0)
        if start == 0:
            copy.wait()
        lanes = pl.ds(start * LANES, (end - start) * LANES)
        blocks = jnp.concatenate([head_ref[:, lanes], tail_ref[:, lanes]], axis=0)
        product = times_transposed(blocks, amp)
        both = product if both is None else both + product
    out_ref[...] = (both[half:, rows:] + both[half:, :rows] + both[:half, rows:]) + both[:half, :rows]


def shards(amplitudes, tile_len, pair_tiles, v_blocks, block_count):
    owners = lax.axis_size("vv")
    slots, window, width = v_blocks.shape[1:]
    stride = owners // slots
    depth = width // LANES
    rows = amplitudes.shape[0]
    arrived = lax.all_to_all(
        amplitudes.reshape(rows, depth, LANES), "vv", split_axis=0, concat_axis=0, tiled=True
    )

    member = lax.axis_index("vv") // stride
    heads, tails = pl.pallas_call(
        split_blocks,
        out_shape=[
            jax.ShapeDtypeStruct((slots * window, width), jnp.bfloat16),
            pltpu.HBM((slots * window, width), jnp.bfloat16),
        ],
        in_specs=[pl.BlockSpec(memory_space=pltpu.SMEM)] * 4 + [pl.BlockSpec(memory_space=pltpu.VMEM)],
        out_specs=[pl.BlockSpec(memory_space=pltpu.VMEM)] * 2,
        compiler_params=pltpu.CompilerParams(vmem_limit_bytes=16 * 1024 * 1024),
        cost_estimate=pl.CostEstimate(
            flops=8 * slots * window * width, bytes_accessed=8 * slots * window * width, transcendentals=0
        ),
        name="split_blocks",
    )(tile_len, pair_tiles, block_count, member.astype(jnp.int32)[None], v_blocks[0])

    terms = pl.pallas_call(
        contract,
        out_shape=jax.ShapeDtypeStruct((slots * window, rows), jnp.float32),
        in_specs=[
            pl.BlockSpec(memory_space=pltpu.VMEM),
            pl.BlockSpec(memory_space=pl.ANY),
            pl.BlockSpec(memory_space=pltpu.VMEM),
        ],
        out_specs=pl.BlockSpec(memory_space=pltpu.VMEM),
        scratch_shapes=[
            pltpu.VMEM((slots * window, width), jnp.bfloat16),
            pltpu.SemaphoreType.DMA,
        ],
        compiler_params=pltpu.CompilerParams(vmem_limit_bytes=16 * 1024 * 1024),
        cost_estimate=pl.CostEstimate(
            flops=8 * slots * window * rows * width, bytes_accessed=6 * rows * width, transcendentals=0
        ),
        name="contract",
    )(heads, pltpu.with_memory_space_constraint(tails, pltpu.HBM), arrived.reshape(rows * depth, LANES))

    groups = [[i + stride * k for k in range(slots)] for i in range(stride)]
    moved = lax.all_to_all(
        terms.reshape(slots, window, rows), "vv", split_axis=0, concat_axis=0, axis_index_groups=groups, tiled=True
    )
    total = (moved[0] + moved[1]) + (moved[2] + moved[3])
    return total.reshape(1, window, 1, rows)


def solution(mesh):
    return jax.shard_map(
        shards,
        mesh=mesh,
        in_specs=(
            P(None, "oo", "vv", None),
            P(),
            P("vv", None),
            P("vv", None, None, None),
            P("vv"),
        ),
        out_specs=P("vv", None, "oo", None),
        check_vma=False,
    )
```

```python
import jax
import jax.numpy as jnp
from jax import lax
from jax.experimental import pallas as pl
from jax.experimental.pallas import tpu as pltpu
from jax.sharding import PartitionSpec as P

TV = 64
LANES = 128
FIRST = 13 / 16


def split_blocks(tile_len_ref, pair_ref, count_ref, member_ref, v_ref, head_ref, tail_ref):
    slots, window, width = v_ref.shape
    c_length = tile_len_ref[pair_ref[0, 0]]
    d_length = tile_len_ref[pair_ref[0, 1]]
    count = count_ref[0]
    member = member_ref[0]
    step = 4 * LANES
    for start in range(0, width, step):
        lanes = pl.ds(start, step)
        index = lax.broadcasted_iota(jnp.int32, (window, step), 1) + start
        inside = (index // TV < c_length) & (index % TV < d_length)
        blocks = []
        for target in range(slots):
            slot = lax.rem(target - member + slots, slots)
            live = jnp.where(slot < count, 1, 0)
            blocks.append(jnp.where(inside & (live > 0), v_ref[slot, :, lanes], 0.0))
        block = jnp.concatenate(blocks, axis=0)
        head = block.astype(jnp.bfloat16)
        head_ref[:, lanes] = head
        tail_ref[:, lanes] = (block - head.astype(jnp.float32)).astype(jnp.bfloat16)


def times_transposed(a, b):
    return lax.dot_general(a, b, (((1,), (1,)), ((), ())), preferred_element_type=jnp.float32)


def contract(head_ref, tail_hbm, amp_ref, out_ref, tail_ref, sem):
    copy = pltpu.make_async_copy(tail_hbm, tail_ref, sem)
    copy.start()
    half, rows = out_ref.shape
    depth = amp_ref.shape[0] // rows
    cut = int(depth * FIRST)
    both = None
    for start, end in ((0, cut), (cut, depth)):
        heads, tails = [], []
        for j in range(start, end):
            part = amp_ref[pl.ds(j, rows, stride=depth), :]
            heads.append(part.astype(jnp.bfloat16))
            tails.append((part - heads[-1].astype(jnp.float32)).astype(jnp.bfloat16))
        amp = jnp.concatenate([jnp.concatenate(heads, axis=1), jnp.concatenate(tails, axis=1)], axis=0)
        if start == 0:
            copy.wait()
        lanes = pl.ds(start * LANES, (end - start) * LANES)
        blocks = jnp.concatenate([head_ref[:, lanes], tail_ref[:, lanes]], axis=0)
        product = times_transposed(blocks, amp)
        both = product if both is None else both + product
    out_ref[...] = (both[half:, rows:] + both[half:, :rows] + both[:half, rows:]) + both[:half, :rows]


def shards(amplitudes, tile_len, pair_tiles, v_blocks, block_count):
    owners = lax.axis_size("vv")
    slots, window, width = v_blocks.shape[1:]
    stride = owners // slots
    depth = width // LANES
    rows = amplitudes.shape[0]
    arrived = lax.all_to_all(
        amplitudes.reshape(rows, depth, LANES), "vv", split_axis=0, concat_axis=0, tiled=True
    )

    member = lax.axis_index("vv") // stride
    heads, tails = pl.pallas_call(
        split_blocks,
        out_shape=[
            jax.ShapeDtypeStruct((slots * window, width), jnp.bfloat16),
            pltpu.HBM((slots * window, width), jnp.bfloat16),
        ],
        in_specs=[pl.BlockSpec(memory_space=pltpu.SMEM)] * 4 + [pl.BlockSpec(memory_space=pltpu.VMEM)],
        out_specs=[pl.BlockSpec(memory_space=pltpu.VMEM)] * 2,
        compiler_params=pltpu.CompilerParams(vmem_limit_bytes=16 * 1024 * 1024),
        cost_estimate=pl.CostEstimate(
            flops=8 * slots * window * width, bytes_accessed=8 * slots * window * width, transcendentals=0
        ),
        name="split_blocks",
    )(tile_len, pair_tiles, block_count, member.astype(jnp.int32)[None], v_blocks[0])

    terms = pl.pallas_call(
        contract,
        out_shape=jax.ShapeDtypeStruct((slots * window, rows), jnp.float32),
        in_specs=[
            pl.BlockSpec(memory_space=pltpu.VMEM),
            pl.BlockSpec(memory_space=pl.ANY),
            pl.BlockSpec(memory_space=pltpu.VMEM),
        ],
        out_specs=pl.BlockSpec(memory_space=pltpu.VMEM),
        scratch_shapes=[
            pltpu.VMEM((slots * window, width), jnp.bfloat16),
            pltpu.SemaphoreType.DMA,
        ],
        compiler_params=pltpu.CompilerParams(vmem_limit_bytes=16 * 1024 * 1024),
        cost_estimate=pl.CostEstimate(
            flops=8 * slots * window * rows * width, bytes_accessed=6 * rows * width, transcendentals=0
        ),
        name="contract",
    )(heads, pltpu.with_memory_space_constraint(tails, pltpu.HBM), arrived.reshape(rows * depth, LANES))

    groups = [[i + stride * k for k in range(slots)] for i in range(stride)]
    moved = lax.all_to_all(
        terms.reshape(slots, window, rows), "vv", split_axis=0, concat_axis=0, axis_index_groups=groups, tiled=True
    )
    total = (moved[0] + moved[1]) + (moved[2] + moved[3])
    return total.reshape(1, window, 1, rows)


def solution(mesh):
    return jax.shard_map(
        shards,
        mesh=mesh,
        in_specs=(
            P(None, "oo", "vv", None),
            P(),
            P("vv", None),
            P("vv", None, None, None),
            P("vv"),
        ),
        out_specs=P("vv", None, "oo", None),
        check_vma=False,
    )
```
